32 devices in a mesh: dp: 4 (over x, core), ctx: 2 (over y), tp: 4 (over z).
Axes of the slice: x: 2, y: 2, z: 4, core: 2. Of those that a mesh axis runs over, the one named last changes fastest.
Arguments:
- query_rows: bfloat16 [2048, 4096], P(('dp', 'ctx'), 'tp'), parts along dimension 0, may hold values from -6 to 6
- key_matrix: bfloat16 [2048, 512], P(('dp', 'ctx'), 'tp'), parts along dimension 0, may hold values from -6 to 6
- value_matrix: bfloat16 [2048, 512], P(('dp', 'ctx'), 'tp'), parts along dimension 0, may hold values from -6 to 6
- attn_out: bfloat16 [2048, 4096], P(('dp', 'ctx'), 'tp'), parts along dimension 0, may hold values from -6 to 6
- out_grad: bfloat16 [2048, 4096], P(('dp', 'ctx', 'tp')), parts along dimension 0, may hold values from -0.5 to 0.5
- log_sums: float32 [32, 2048], P('tp', ('dp', 'ctx')), parts along dimension 1, may hold values from 3 to 5
- block_mask: int32 [16, 4], P('dp'), parts along dimension 0, may hold values 0 or 1
Outputs:
- query_grad: bfloat16 [2048, 4096], P(('dp', 'ctx'), 'tp'), parts along dimension 0
- key_gradient: bfloat16 [2048, 512], P(('dp', 'ctx'), 'tp'), parts along dimension 0
- value_gradient: bfloat16 [2048, 512], P(('dp', 'ctx'), 'tp'), parts along dimension 0
The draws below stay inside these ranges and needn't reach their ends.
There are 4 independent parts, one for each index of `dp`. The reference program is written for one: setup_inputs(seed, part) draws one part's arguments, and reference() takes and returns one part's arrays. A program takes and returns all parts, laid end to end along the dimension named above; each array names one. Nothing has to cross between parts.
Inputs may be any that keep to these rules, and one draw needn't show every extreme that they name: `block_mask`: entry [a, b] with b < a lets query block a see key block b; entries on and above the diagonal are never read.
All inputs are finite; a program needn't handle non-finite values.
Results may differ from the reference program's by a relative error of at most 0.0049.
Values may be sent and summed in bfloat16 or wider, within the bound.
A program may use at most 64 MiB of HBM per device.

```python
import math
import jax
import jax.numpy as jnp
from jax import lax

BLK = 128
HEAD_SIZE = 128
QUERY_PER_KEY = 8
KEY_VALUE_HEADS = 4
HQ = 32
TOKEN_COUNT = 512
NB = 4


def place_ends(result, own_key, smallest, high):
    spot = [jax.random.randint(jax.random.fold_in(own_key, axis), (), 0, length) for axis, length in enumerate(result.shape)]
    widest = result.shape.index(max(result.shape))
    neighbour = spot[:widest] + [(spot[widest] + 1) % result.shape[widest]] + spot[widest + 1:]
    return result.at[tuple(spot)].set(smallest).at[tuple(neighbour)].set(high)


def levels(stream_key, dims, cuts, least, largest):
    factor_of = 1.0
    for position, parts in cuts:
        steps = jax.random.uniform(jax.random.fold_in(jax.random.fold_in(stream_key, 6), position), (parts,), jnp.float32, least / len(cuts), largest / len(cuts))
        factor_of = factor_of * jnp.repeat(jnp.exp(steps), dims[position] // parts).reshape((-1,) + (1,) * (len(dims) - 1 - position))
    return factor_of


def bell_draw(own_key, shape, spread, most, cuts=(), held_as=jnp.bfloat16):
    drawn = jax.random.normal(own_key, shape, jnp.float32) * spread
    if len(cuts) > 0:
        drawn = levels(own_key, shape, cuts, -0.22, 0.18) * drawn
    return jnp.clip(drawn, min=-most, max=most).astype(held_as)


def setup_inputs(seed: int = 0, part: int = 0) -> dict:
    seeds = jax.random.split(jax.random.key(seed), 8)
    part_splits = jax.random.split(jax.random.fold_in(seeds[7], part), 8)
    query_rows = bell_draw(part_splits[0], (TOKEN_COUNT, HQ * HEAD_SIZE), 1.0, 6.0, ((0, 2), (1, 4)))
    key_matrix = bell_draw(part_splits[1], (TOKEN_COUNT, KEY_VALUE_HEADS * HEAD_SIZE), 1.0, 6.0, ((0, 2), (1, 4)))
    value_matrix = bell_draw(part_splits[2], (TOKEN_COUNT, KEY_VALUE_HEADS * HEAD_SIZE), 1.0, 6.0, ((0, 2), (1, 4)))
    attn_out = bell_draw(part_splits[3], (TOKEN_COUNT, HQ * HEAD_SIZE), 1.0, 6.0, ((0, 2), (1, 4)))
    out_grad = bell_draw(part_splits[4], (TOKEN_COUNT, HQ * HEAD_SIZE), HEAD_SIZE ** -0.5, 0.5, ((0, 8),))
    log_sums = jnp.clip(3.0 + 2.0 * jax.random.uniform(part_splits[5], (HQ, TOKEN_COUNT), jnp.float32) ** levels(part_splits[5], (HQ, TOKEN_COUNT), ((0, 4), (1, 2)), -0.2, 0.2), 3.0, 5.0)
    block_mask = place_ends((jax.random.randint(part_splits[6], (NB, NB), 0, 4) < 3).astype(jnp.int32), jax.random.fold_in(part_splits[6], 1), 0, 1)
    return dict(query_rows=query_rows, key_matrix=key_matrix, value_matrix=value_matrix, attn_out=attn_out, out_grad=out_grad, log_sums=log_sums, block_mask=block_mask)


def reference(query_rows, key_matrix, value_matrix, attn_out, out_grad, log_sums, block_mask):
    logit_scale = 1.0 / math.sqrt(HEAD_SIZE)
    queries = query_rows.reshape(TOKEN_COUNT, HQ, HEAD_SIZE).astype(jnp.float32)
    grad_heads = out_grad.reshape(TOKEN_COUNT, HQ, HEAD_SIZE).astype(jnp.float32)
    outputs = attn_out.reshape(TOKEN_COUNT, HQ, HEAD_SIZE).astype(jnp.float32)
    row_delta = lax.optimization_barrier(jnp.sum(grad_heads * outputs, axis=2))
    keys_expanded = jnp.repeat(key_matrix.reshape(TOKEN_COUNT, KEY_VALUE_HEADS, HEAD_SIZE).astype(jnp.float32), QUERY_PER_KEY, axis=1)
    values_expanded = jnp.repeat(value_matrix.reshape(TOKEN_COUNT, KEY_VALUE_HEADS, HEAD_SIZE).astype(jnp.float32), QUERY_PER_KEY, axis=1)
    key_pos = jnp.arange(TOKEN_COUNT, dtype=jnp.int32)
    key_block = key_pos // BLK

    def tile_step(carried, block_index):
        key_running_total, value_running_total = carried
        row_start = block_index * BLK
        query_tile = lax.dynamic_slice_in_dim(queries, row_start, BLK, 0)
        grad_tile = lax.dynamic_slice_in_dim(grad_heads, row_start, BLK, 0)
        delta_tile = lax.dynamic_slice_in_dim(row_delta, row_start, BLK, 0)
        lse_tile = lax.dynamic_slice_in_dim(log_sums, row_start, BLK, 1)
        mask_row = lax.dynamic_index_in_dim(block_mask, block_index, 0, keepdims=False)
        allowed = mask_row[key_block]
        query_pos = row_start + jnp.arange(BLK, dtype=jnp.int32)
        earlier = ((key_block < block_index) & (allowed == 1))[None, :]
        diagonal = (key_block == block_index)[None, :] & (key_pos[None, :] <= query_pos[:, None])
        live_mask = earlier | diagonal
        scores = jnp.einsum('ihd,jhd->hij', query_tile, keys_expanded) * logit_scale
        probabilities = jnp.where(live_mask[None], jnp.exp(scores - lse_tile[:, :, None]), 0.0)
        prob_grad = jnp.einsum('ihd,jhd->hij', grad_tile, values_expanded)
        dscore = probabilities * (prob_grad - delta_tile.T[:, :, None])
        dscore = lax.optimization_barrier(dscore.astype(jnp.bfloat16)).astype(jnp.float32)
        rounded = lax.optimization_barrier(probabilities.astype(jnp.bfloat16)).astype(jnp.float32)
        query_term = jnp.einsum('hij,jhd->ihd', dscore, keys_expanded) * logit_scale
        key_running_total = key_running_total + jnp.einsum('hij,ihd->jhd', dscore, query_tile)
        value_running_total = value_running_total + jnp.einsum('hij,ihd->jhd', rounded, grad_tile)
        return ((key_running_total, value_running_total), query_term)
    zero_grad = jnp.zeros((TOKEN_COUNT, HQ, HEAD_SIZE), jnp.float32)
    (key_running_total, value_running_total), query_tiles = lax.scan(tile_step, (zero_grad, zero_grad), jnp.arange(NB, dtype=jnp.int32))
    query_grad = query_tiles.reshape(TOKEN_COUNT, HQ * HEAD_SIZE).astype(jnp.bfloat16)
    key_gradient_sum = lax.optimization_barrier(jnp.sum(key_running_total.reshape(TOKEN_COUNT, KEY_VALUE_HEADS, QUERY_PER_KEY, HEAD_SIZE), axis=2)) * logit_scale
    value_gradient_sum = lax.optimization_barrier(jnp.sum(value_running_total.reshape(TOKEN_COUNT, KEY_VALUE_HEADS, QUERY_PER_KEY, HEAD_SIZE), axis=2))
    key_gradient = key_gradient_sum.reshape(TOKEN_COUNT, KEY_VALUE_HEADS * HEAD_SIZE).astype(jnp.bfloat16)
    value_gradient = value_gradient_sum.reshape(TOKEN_COUNT, KEY_VALUE_HEADS * HEAD_SIZE).astype(jnp.bfloat16)
    return (query_grad, key_gradient, value_gradient)
```

```python
import functools
import math

import jax
import jax.numpy as jnp
from jax import lax
from jax.experimental import pallas as pl
from jax.experimental.pallas import tpu as pltpu
from jax.sharding import PartitionSpec as P

BLK = 128
HEAD_SIZE = 128
MESH = pl.DeviceIdType.MESH
BF16 = jnp.bfloat16
F32 = jnp.float32


def dot(a, b, dims=((1,), (0,))):
    return lax.dot_general(a, b, (dims, ((), ())), preferred_element_type=F32)


def partner(me, k, count):
    if count == 4:
        if k == 1:
            return me + 1 - 2 * lax.rem(me, 2)
        if k == 2:
            return lax.rem(me + 2, 4)
        return 3 - me
    return lax.rem(me + k, count)


def source_of(me, k, count):
    if count == 4:
        return partner(me, k, count)
    return lax.rem(me + count - k, count)


def kernel(
    n, tp,
    q_hbm, k_hbm, v_hbm, o_hbm, g_hbm, lse_hbm, mask_ref,
    dq_hbm, dk_hbm, dv_hbm,
    q, o, g, lse, kb, vb, vx, lcol, lhs, p, pt, qt, dq_acc, dq_st, dkt, dva,
    dk_send, dv_send, dk_recv, dv_recv, dk_st, dv_st,
    load_sem, out_sem, g_send, g_recv, kv_send, kv_recv, d_send, d_recv,
):
    c = lax.axis_index("ctx")
    me = lax.axis_index("tp")
    tokens = q.shape[0]
    heads = q.shape[1] // HEAD_SIZE
    rows = tokens // tp
    span_blocks = tokens // BLK
    chunk_per_block = BLK // rows
    width = heads * HEAD_SIZE
    scale = 1.0 / math.sqrt(HEAD_SIZE)

    def chunk_rows(s):
        return pl.ds(pl.multiple_of(s * rows, rows), rows)

    loads = [
        pltpu.make_async_copy(src, dst, load_sem.at[i])
        for i, (src, dst) in enumerate(
            [
                (q_hbm, q),
                (k_hbm, kb.at[0]),
                (lse_hbm, lse),
                (v_hbm, vb.at[0]),
                (o_hbm, o),
                (
                    g_hbm.at[:, pl.ds(pl.multiple_of(me * width, width), width)],
                    g.at[chunk_rows(me)],
                ),
            ]
        )
    ]
    for load in loads:
        load.start()

    barrier = pltpu.get_barrier_semaphore()
    for k in range(1, tp):
        pl.semaphore_signal(
            barrier, inc=1, device_id={"tp": lax.rem(me + k, tp)}, device_id_type=MESH
        )
    for d in range(1, n):
        pl.semaphore_signal(
            barrier, inc=1, device_id={"ctx": lax.rem(c + d, n)}, device_id_type=MESH
        )
    pl.semaphore_wait(barrier, tp - 1 + n - 1)

    def grad_copy(k):
        to = partner(me, k, tp)
        return pltpu.make_async_remote_copy(
            src_ref=g_hbm.at[:, pl.ds(pl.multiple_of(to * width, width), width)],
            dst_ref=g.at[chunk_rows(me)],
            send_sem=g_send.at[k - 1],
            recv_sem=g_recv.at[k - 1],
            device_id={"tp": to},
            device_id_type=MESH,
        )

    def grad_arrival(k):
        return pltpu.make_async_remote_copy(
            src_ref=g_hbm.at[:, pl.ds(0, width)],
            dst_ref=g.at[chunk_rows(source_of(me, k, tp))],
            send_sem=g_send.at[k - 1],
            recv_sem=g_recv.at[k - 1],
            device_id={"tp": source_of(me, k, tp)},
            device_id_type=MESH,
        )

    order = (2, 3, 1) if tp == 4 else tuple(range(1, tp))
    for k in order:
        grad_copy(k).start()

    def kv_copies(d):
        to = lax.rem(c + d, n)
        return [
            pltpu.make_async_remote_copy(
                src_ref=src,
                dst_ref=dst.at[d],
                send_sem=kv_send.at[i, d - 1],
                recv_sem=kv_recv.at[i, d - 1],
                device_id={"ctx": to},
                device_id_type=MESH,
            )
            for i, (src, dst) in enumerate([(k_hbm, kb), (v_hbm, vb)])
        ]

    for d in range(1, n):

        @pl.when(c + d < n)
        def _():
            for copy in kv_copies(d):
                copy.start()

    def stack(ref, s):
        return jnp.concatenate(
            [
                ref[chunk_rows(s), h * HEAD_SIZE : (h + 1) * HEAD_SIZE]
                for h in range(heads)
            ],
            axis=0,
        )

    def span_probs(slot, d, own):
        keys = kb[d]
        vx[slot, :, 0:HEAD_SIZE] = vb[d]
        key_at = lax.broadcasted_iota(jnp.int32, (rows, tokens), 1)
        row_at = lax.broadcasted_iota(jnp.int32, (rows, tokens), 0)
        key_block = key_at // BLK
        for s in range(tp):
            block = s // chunk_per_block
            table = jnp.zeros((rows, tokens), jnp.int32)
            for b in range(span_blocks if not own else block):
                allowed = mask_ref[c * span_blocks + block, (c - d) * span_blocks + b]
                table = jnp.where(key_block == b, allowed, table)
            live = table == 1
            if own:
                live = live | ((key_block == block) & (key_at <= row_at + s * rows))
            scores = dot(stack(q, s), keys, ((1,), (1,)))
            for h in range(heads):
                part = scores[h * rows : (h + 1) * rows] * scale
                col = lcol[s * rows : (s + 1) * rows, h : h + 1]
                p[slot, s, h * rows : (h + 1) * rows, :] = jnp.where(
                    live, jnp.exp(part - col), 0.0
                )
            pt[slot, s] = p[slot, s].T.astype(BF16)

    def chunk_lhs(s):
        grads = stack(g, s)
        product = grads.astype(F32) * stack(o, s).astype(F32)
        high = product.astype(BF16)
        low = (product - high.astype(F32)).astype(BF16)
        lhs[s] = jnp.concatenate([grads, high, low], axis=1)

    def chunk_terms(slot, d, s):
        inner = dot(lhs[s], vx[slot], ((1,), (1,)))
        dscore = (p[slot, s] * inner).astype(BF16)
        dkt[slot] += dot(qt[s], dscore)
        dva[slot] += dot(pt[slot, s], lhs[s, :, 0:HEAD_SIZE])
        return dot(dscore, kb[d])

    def out_copy(s, i):
        return pltpu.make_async_copy(
            dq_st.at[chunk_rows(s)], dq_hbm.at[chunk_rows(s)], out_sem.at[i]
        )

    def finish_query(s, total, i):
        grad = (total * scale).astype(BF16)
        for h in range(heads):
            dq_st[chunk_rows(s), h * HEAD_SIZE : (h + 1) * HEAD_SIZE] = grad[
                h * rows : (h + 1) * rows
            ]
        out_copy(s, i).start()

    def partial_copies(d):
        to = lax.rem(c - d + n, n)
        return [
            pltpu.make_async_remote_copy(
                src_ref=src.at[d - 1],
                dst_ref=dst.at[d - 1],
                send_sem=d_send.at[i, d - 1],
                recv_sem=d_recv.at[i, d - 1],
                device_id={"ctx": to},
                device_id_type=MESH,
            )
            for i, (src, dst) in enumerate([(dk_send, dk_recv), (dv_send, dv_recv)])
        ]

    def send_partials(d):
        dk_send[d - 1] = dkt[1].astype(BF16)
        dv_send[d - 1] = dva[1].astype(BF16)
        for copy in partial_copies(d):
            copy.start()

    dkt[...] = jnp.zeros_like(dkt)
    dva[...] = jnp.zeros_like(dva)
    dq_acc[...] = jnp.zeros_like(dq_acc)
    vx[:, :, HEAD_SIZE:] = jnp.full((2, tokens, 2 * HEAD_SIZE), -1.0, BF16)
    for load in loads:
        load.wait()
    lcol[...] = lse[...].T
    for s in range(tp):
        qt[s] = stack(q, s).T
    span_probs(0, 0, True)

    @pl.when(c >= 1)
    def _():
        for copy in kv_copies(1):
            copy.wait_recv()
        span_probs(1, 1, False)

    steps = (0,) + ((1, 2, 3) if tp == 4 else tuple(range(1, tp)))
    for i, k in enumerate(steps):
        if k == 0:
            s = me
        else:
            s = source_of(me, k, tp)
            grad_arrival(k).wait_recv()
        chunk_lhs(s)

        @pl.when(c >= 1)
        def _():
            dq_acc[s] += chunk_terms(1, 1, s)
            if i == tp - 1:
                send_partials(1)

        total = dq_acc[s] + chunk_terms(0, 0, s)
        if n == 2:
            finish_query(s, total, i)
        else:
            dq_acc[s] = total

    if n > 2:

        @pl.loop(2, n)
        def _(d):
            @pl.when(c >= d)
            def _():
                for copy in kv_copies(d):
                    copy.wait_recv()
                dkt[1] = jnp.zeros(dkt.shape[1:], F32)
                dva[1] = jnp.zeros(dva.shape[1:], F32)
                span_probs(1, d, False)
                for s in range(tp):
                    dq_acc[s] += chunk_terms(1, d, s)
                send_partials(d)

        for s in range(tp):
            finish_query(s, dq_acc[s], s)

    for d in range(1, n):

        @pl.when(c + d < n)
        def _():
            for copy in partial_copies(d):
                copy.wait_recv()
            dkt[0] += dk_recv[d - 1].astype(F32)
            dva[0] += dv_recv[d - 1].astype(F32)

    dk_st[...] = (dkt[0] * scale).T.astype(BF16)
    dv_st[...] = dva[0].astype(BF16)
    ends = [
        pltpu.make_async_copy(dk_st, dk_hbm, out_sem.at[tp]),
        pltpu.make_async_copy(dv_st, dv_hbm, out_sem.at[tp + 1]),
    ]
    for copy in ends:
        copy.start()

    for k in range(1, tp):
        grad_copy(k).wait_send()
    for d in range(1, n):

        @pl.when(c + d < n)
        def _():
            for copy in kv_copies(d):
                copy.wait_send()

        @pl.when(c >= d)
        def _():
            for copy in partial_copies(d):
                copy.wait_send()

    for i, k in enumerate(steps):
        if n == 2:
            out_copy(me if k == 0 else source_of(me, k, tp), i).wait()
        else:
            out_copy(i, i).wait()
    for copy in ends:
        copy.wait()


def local(query_rows, key_matrix, value_matrix, attn_out, out_grad, log_sums, block_mask):
    tokens, width = query_rows.shape
    heads = width // HEAD_SIZE
    n = lax.axis_size("ctx")
    tp = lax.axis_size("tp")
    rows = tokens // tp
    stacked = heads * rows
    vmem = pltpu.VMEM
    dma = pltpu.SemaphoreType.DMA
    anywhere = pl.BlockSpec(memory_space=pl.ANY)
    return pl.pallas_call(
        functools.partial(kernel, n, tp),
        out_shape=(
            jax.ShapeDtypeStruct((tokens, width), BF16),
            jax.ShapeDtypeStruct((tokens, HEAD_SIZE), BF16),
            jax.ShapeDtypeStruct((tokens, HEAD_SIZE), BF16),
        ),
        in_specs=[anywhere] * 6 + [pl.BlockSpec(memory_space=pltpu.SMEM)],
        out_specs=(anywhere,) * 3,
        scratch_shapes=[
            vmem((tokens, width), BF16),
            vmem((tokens, width), BF16),
            vmem((tokens, width), BF16),
            vmem((heads, tokens), F32),
            vmem((n, tokens, HEAD_SIZE), BF16),
            vmem((n, tokens, HEAD_SIZE), BF16),
            vmem((2, tokens, 3 * HEAD_SIZE), BF16),
            vmem((tokens, heads), F32),
            vmem((tp, stacked, 3 * HEAD_SIZE), BF16),
            vmem((2, tp, stacked, tokens), F32),
            vmem((2, tp, tokens, stacked), BF16),
            vmem((tp, HEAD_SIZE, stacked), BF16),
            vmem((tp, stacked, HEAD_SIZE), F32),
            vmem((tokens, width), BF16),
            vmem((2, HEAD_SIZE, tokens), F32),
            vmem((2, tokens, HEAD_SIZE), F32),
            vmem((n - 1, HEAD_SIZE, tokens), BF16),
            vmem((n - 1, tokens, HEAD_SIZE), BF16),
            vmem((n - 1, HEAD_SIZE, tokens), BF16),
            vmem((n - 1, tokens, HEAD_SIZE), BF16),
            vmem((tokens, HEAD_SIZE), BF16),
            vmem((tokens, HEAD_SIZE), BF16),
            dma((6,)),
            dma((tp + 2,)),
            dma((tp - 1,)),
            dma((tp - 1,)),
            dma((2, n - 1)),
            dma((2, n - 1)),
            dma((2, n - 1)),
            dma((2, n - 1)),
        ],
        compiler_params=pltpu.CompilerParams(
            collective_id=0, has_side_effects=True, vmem_limit_bytes=48 * 1024 * 1024
        ),
    )(query_rows, key_matrix, value_matrix, attn_out, out_grad, log_sums, block_mask)


def solution(mesh):
    placed = (
        P(("dp", "ctx"), "tp"),
        P(("dp", "ctx"), "tp"),
        P(("dp", "ctx"), "tp"),
        P(("dp", "ctx"), "tp"),
        P(("dp", "ctx", "tp"), None),
        P("tp", ("dp", "ctx")),
        P("dp", None),
    )
    return jax.shard_map(
        local,
        mesh=mesh,
        in_specs=placed,
        out_specs=(P(("dp", "ctx"), "tp"), P(("dp", "ctx"), "tp"), P(("dp", "ctx"), "tp")),
        check_vma=False,
    )
```

```python
import functools
import math

import jax
import jax.numpy as jnp
from jax import lax
from jax.experimental import pallas as pl
from jax.experimental.pallas import tpu as pltpu
from jax.sharding import PartitionSpec as P

BLK = 128
HEAD_SIZE = 128
MESH = pl.DeviceIdType.MESH
BF16 = jnp.bfloat16
F32 = jnp.float32


def dot(a, b, dims=((1,), (0,))):
    return lax.dot_general(a, b, (dims, ((), ())), preferred_element_type=F32)


def partner(me, k, count):
    if count == 4:
        if k == 1:
            return me + 1 - 2 * lax.rem(me, 2)
        if k == 2:
            return lax.rem(me + 2, 4)
        return 3 - me
    return lax.rem(me + k, count)


def source_of(me, k, count):
    if count == 4:
        return partner(me, k, count)
    return lax.rem(me + count - k, count)


def kernel(
    n, tp,
    q_hbm, k_hbm, v_hbm, o_hbm, g_hbm, lse_hbm, mask_hbm,
    dq_st, dk_st, dv_st,
    q, o, g, lse, kb, vb, vx, lcol, lhs, p, pt, qt, dq_acc, dkt, dva,
    dk_send, dv_send, dk_recv, dv_recv, mask_ref,
    load_sem, g_send, g_recv, kv_send, kv_recv, d_send, d_recv,
):
    c = lax.axis_index("ctx")
    me = lax.axis_index("tp")
    tokens = q.shape[0]
    heads = q.shape[1] // HEAD_SIZE
    rows = tokens // tp
    span_blocks = tokens // BLK
    chunk_per_block = BLK // rows
    width = heads * HEAD_SIZE
    scale = 1.0 / math.sqrt(HEAD_SIZE)

    def chunk_rows(s):
        return pl.ds(pl.multiple_of(s * rows, rows), rows)

    loads = [
        pltpu.make_async_copy(src, dst, load_sem.at[i])
        for i, (src, dst) in enumerate(
            [
                (mask_hbm, mask_ref),
                (q_hbm, q),
                (k_hbm, kb.at[0]),
                (lse_hbm, lse),
                (v_hbm, vb.at[0]),
                (o_hbm, o),
                (
                    g_hbm.at[:, pl.ds(pl.multiple_of(me * width, width), width)],
                    g.at[chunk_rows(me)],
                ),
            ]
        )
    ]
    for load in loads:
        load.start()

    barrier = pltpu.get_barrier_semaphore()
    for k in range(1, tp):
        pl.semaphore_signal(
            barrier, inc=1, device_id={"tp": lax.rem(me + k, tp)}, device_id_type=MESH
        )
    for d in range(1, n):
        pl.semaphore_signal(
            barrier, inc=1, device_id={"ctx": lax.rem(c + d, n)}, device_id_type=MESH
        )
    pl.semaphore_wait(barrier, tp - 1 + n - 1)

    def grad_copy(k):
        to = partner(me, k, tp)
        return pltpu.make_async_remote_copy(
            src_ref=g_hbm.at[:, pl.ds(pl.multiple_of(to * width, width), width)],
            dst_ref=g.at[chunk_rows(me)],
            send_sem=g_send.at[k - 1],
            recv_sem=g_recv.at[k - 1],
            device_id={"tp": to},
            device_id_type=MESH,
        )

    def grad_arrival(k):
        return pltpu.make_async_remote_copy(
            src_ref=g_hbm.at[:, pl.ds(0, width)],
            dst_ref=g.at[chunk_rows(source_of(me, k, tp))],
            send_sem=g_send.at[k - 1],
            recv_sem=g_recv.at[k - 1],
            device_id={"tp": source_of(me, k, tp)},
            device_id_type=MESH,
        )

    order = (1, 2, 3) if tp == 4 else tuple(range(1, tp))
    for k in order:
        grad_copy(k).start()

    def kv_copies(d):
        to = lax.rem(c + d, n)
        return [
            pltpu.make_async_remote_copy(
                src_ref=src,
                dst_ref=dst.at[d],
                send_sem=kv_send.at[i, d - 1],
                recv_sem=kv_recv.at[i, d - 1],
                device_id={"ctx": to},
                device_id_type=MESH,
            )
            for i, (src, dst) in enumerate([(k_hbm, kb), (v_hbm, vb)])
        ]

    for d in range(1, n):

        @pl.when(c + d < n)
        def _():
            for copy in kv_copies(d):
                copy.start()

    def stack(ref, s):
        return jnp.concatenate(
            [
                ref[chunk_rows(s), h * HEAD_SIZE : (h + 1) * HEAD_SIZE]
                for h in range(heads)
            ],
            axis=0,
        )

    def span_probs(slot, d, own):
        keys = kb[d]
        vx[slot, :, 0:HEAD_SIZE] = vb[d]
        key_at = lax.broadcasted_iota(jnp.int32, (rows, tokens), 1)
        row_at = lax.broadcasted_iota(jnp.int32, (rows, tokens), 0)
        key_block = key_at // BLK
        for s in range(tp):
            block = s // chunk_per_block
            table = jnp.zeros((rows, tokens), jnp.int32)
            for b in range(span_blocks if not own else block):
                allowed = mask_ref[c * span_blocks + block, (c - d) * span_blocks + b]
                table = jnp.where(key_block == b, allowed, table)
            live = table == 1
            if own:
                live = live | ((key_block == block) & (key_at <= row_at + s * rows))
            scores = dot(stack(q, s), keys, ((1,), (1,)))
            for h in range(heads):
                part = scores[h * rows : (h + 1) * rows] * scale
                col = lcol[s * rows : (s + 1) * rows, h : h + 1]
                p[slot, s, h * rows : (h + 1) * rows, :] = jnp.where(
                    live, jnp.exp(part - col), 0.0
                )
            pt[slot, s] = p[slot, s].T.astype(BF16)

    def chunk_lhs(s, grads):
        product = grads.astype(F32) * stack(o, s).astype(F32)
        high = product.astype(BF16)
        low = (product - high.astype(F32)).astype(BF16)
        lhs[s] = jnp.concatenate([grads, high, low], axis=1)

    def value_term(slot, s, grads):
        dva[slot] += dot(pt[slot, s], grads)

    def key_term(slot, s):
        inner = dot(lhs[s], vx[slot], ((1,), (1,)))
        dscore = (p[slot, s] * inner).astype(BF16)
        dkt[slot] += dot(qt[s], dscore)
        return dscore

    def chunk_terms(slot, d, s):
        value_term(slot, s, lhs[s, :, 0:HEAD_SIZE])
        return dot(key_term(slot, s), kb[d])

    def finish_query(s, total):
        grad = (total * scale).astype(BF16)
        for h in range(heads):
            dq_st[chunk_rows(s), h * HEAD_SIZE : (h + 1) * HEAD_SIZE] = grad[
                h * rows : (h + 1) * rows
            ]

    def partial_copies(d):
        to = lax.rem(c - d + n, n)
        return [
            pltpu.make_async_remote_copy(
                src_ref=src.at[d - 1],
                dst_ref=dst.at[d - 1],
                send_sem=d_send.at[i, d - 1],
                recv_sem=d_recv.at[i, d - 1],
                device_id={"ctx": to},
                device_id_type=MESH,
            )
            for i, (src, dst) in enumerate([(dk_send, dk_recv), (dv_send, dv_recv)])
        ]

    def send_value_partial(d):
        dv_send[d - 1] = dva[1].astype(BF16)
        partial_copies(d)[1].start()

    def send_key_partial(d):
        dk_send[d - 1] = dkt[1].astype(BF16)
        partial_copies(d)[0].start()

    dkt[...] = jnp.zeros_like(dkt)
    dva[...] = jnp.zeros_like(dva)
    dq_acc[...] = jnp.zeros_like(dq_acc)
    vx[:, :, HEAD_SIZE:] = jnp.full((2, tokens, 2 * HEAD_SIZE), -1.0, BF16)
    for load in loads:
        load.wait()
    lcol[...] = lse[...].T
    for s in range(tp):
        qt[s] = stack(q, s).T
    span_probs(0, 0, True)

    @pl.when(c >= 1)
    def _():
        for copy in kv_copies(1):
            copy.wait_recv()
        span_probs(1, 1, False)

    steps = (0,) + ((1, 2, 3) if tp == 4 else tuple(range(1, tp)))
    for i, k in enumerate(steps):
        if k == 0:
            s = me
        else:
            s = source_of(me, k, tp)
            grad_arrival(k).wait_recv()
        grads = stack(g, s)
        if i < tp - 1:
            chunk_lhs(s, grads)

            @pl.when(c >= 1)
            def _():
                dq_acc[s] += chunk_terms(1, 1, s)

        else:
            @pl.when(c >= 1)
            def _():
                value_term(1, s, grads)
                send_value_partial(1)

            chunk_lhs(s, grads)

            @pl.when(c >= 1)
            def _():
                dscore = key_term(1, s)
                send_key_partial(1)
                dq_acc[s] += dot(dscore, kb[1])

        total = dq_acc[s] + chunk_terms(0, 0, s)
        if n == 2:
            finish_query(s, total)
        else:
            dq_acc[s] = total

    if n > 2:

        @pl.loop(2, n)
        def _(d):
            @pl.when(c >= d)
            def _():
                for copy in kv_copies(d):
                    copy.wait_recv()
                dkt[1] = jnp.zeros(dkt.shape[1:], F32)
                dva[1] = jnp.zeros(dva.shape[1:], F32)
                span_probs(1, d, False)
                for s in range(tp):
                    dq_acc[s] += chunk_terms(1, d, s)
                send_value_partial(d)
                send_key_partial(d)

        for s in range(tp):
            finish_query(s, dq_acc[s])

    for d in range(1, n):

        @pl.when(c + d < n)
        def _():
            keys_in, values_in = partial_copies(d)
            values_in.wait_recv()
            dva[0] += dv_recv[d - 1].astype(F32)
            keys_in.wait_recv()
            dkt[0] += dk_recv[d - 1].astype(F32)

    dk_st[...] = (dkt[0] * scale).T.astype(BF16)
    dv_st[...] = dva[0].astype(BF16)
    for k in range(1, tp):
        grad_copy(k).wait_send()
    for d in range(1, n):

        @pl.when(c + d < n)
        def _():
            for copy in kv_copies(d):
                copy.wait_send()

        @pl.when(c >= d)
        def _():
            for copy in partial_copies(d):
                copy.wait_send()


def local(query_rows, key_matrix, value_matrix, attn_out, out_grad, log_sums, block_mask):
    tokens, width = query_rows.shape
    heads = width // HEAD_SIZE
    n = lax.axis_size("ctx")
    tp = lax.axis_size("tp")
    rows = tokens // tp
    stacked = heads * rows
    vmem = pltpu.VMEM
    dma = pltpu.SemaphoreType.DMA
    hbm = pl.BlockSpec(memory_space=pltpu.HBM)
    return pl.pallas_call(
        functools.partial(kernel, n, tp),
        out_shape=(
            vmem((tokens, width), BF16),
            vmem((tokens, HEAD_SIZE), BF16),
            vmem((tokens, HEAD_SIZE), BF16),
        ),
        in_specs=[hbm] * 7,
        out_specs=(pl.BlockSpec(memory_space=pltpu.VMEM),) * 3,
        scratch_shapes=[
            vmem((tokens, width), BF16),
            vmem((tokens, width), BF16),
            vmem((tokens, width), BF16),
            vmem((heads, tokens), F32),
            vmem((n, tokens, HEAD_SIZE), BF16),
            vmem((n, tokens, HEAD_SIZE), BF16),
            vmem((2, tokens, 3 * HEAD_SIZE), BF16),
            vmem((tokens, heads), F32),
            vmem((tp, stacked, 3 * HEAD_SIZE), BF16),
            vmem((2, tp, stacked, tokens), F32),
            vmem((2, tp, tokens, stacked), BF16),
            vmem((tp, HEAD_SIZE, stacked), BF16),
            vmem((tp, stacked, HEAD_SIZE), F32),
            vmem((2, HEAD_SIZE, tokens), F32),
            vmem((2, tokens, HEAD_SIZE), F32),
            vmem((n - 1, HEAD_SIZE, tokens), BF16),
            vmem((n - 1, tokens, HEAD_SIZE), BF16),
            vmem((n - 1, HEAD_SIZE, tokens), BF16),
            vmem((n - 1, tokens, HEAD_SIZE), BF16),
            pltpu.SMEM(block_mask.shape, jnp.int32),
            dma((7,)),
            dma((tp - 1,)),
            dma((tp - 1,)),
            dma((2, n - 1)),
            dma((2, n - 1)),
            dma((2, n - 1)),
            dma((2, n - 1)),
        ],
        compiler_params=pltpu.CompilerParams(
            collective_id=0, has_side_effects=True, vmem_limit_bytes=62 * 1024 * 1024
        ),
    )(query_rows, key_matrix, value_matrix, attn_out, out_grad, log_sums, block_mask)


def solution(mesh):
    placed = (
        P(("dp", "ctx"), "tp"),
        P(("dp", "ctx"), "tp"),
        P(("dp", "ctx"), "tp"),
        P(("dp", "ctx"), "tp"),
        P(("dp", "ctx", "tp"), None),
        P("tp", ("dp", "ctx")),
        P("dp", None),
    )
    return jax.shard_map(
        local,
        mesh=mesh,
        in_specs=placed,
        out_specs=(P(("dp", "ctx"), "tp"), P(("dp", "ctx"), "tp"), P(("dp", "ctx"), "tp")),
        check_vma=False,
    )
```

```python
import functools
import math

import jax
import jax.numpy as jnp
from jax import lax
from jax.experimental import pallas as pl
from jax.experimental.pallas import tpu as pltpu
from jax.sharding import PartitionSpec as P

BLK = 128
HEAD_SIZE = 128
MESH = pl.DeviceIdType.MESH
BF16 = jnp.bfloat16
F32 = jnp.float32


def dot(a, b, dims=((1,), (0,))):
    return lax.dot_general(a, b, (dims, ((), ())), preferred_element_type=F32)


def partner(me, k, count):
    if count == 4:
        if k == 1:
            return me + 1 - 2 * lax.rem(me, 2)
        if k == 2:
            return lax.rem(me + 2, 4)
        return 3 - me
    return lax.rem(me + k, count)


def source_of(me, k, count):
    if count == 4:
        return partner(me, k, count)
    return lax.rem(me + count - k, count)


def kernel(
    n, tp,
    q_hbm, k_hbm, v_hbm, o_hbm, g_hbm, lse_hbm, mask_hbm,
    dq_st, dk_st, dv_st,
    q, o, g, lse, kb, vb, vx, lcol, lhs, p, pt, qt, dq_acc, dkt, dva,
    dk_send, dv_send, dk_recv, dv_recv, mask_ref,
    load_sem, g_send, g_recv, kv_send, kv_recv, d_send, d_recv,
):
    c = lax.axis_index("ctx")
    me = lax.axis_index("tp")
    tokens = q.shape[0]
    heads = q.shape[1] // HEAD_SIZE
    rows = tokens // tp
    span_blocks = tokens // BLK
    chunk_per_block = BLK // rows
    width = heads * HEAD_SIZE
    scale = 1.0 / math.sqrt(HEAD_SIZE)

    def chunk_rows(s):
        return pl.ds(pl.multiple_of(s * rows, rows), rows)

    loads = [
        pltpu.make_async_copy(src, dst, load_sem.at[i])
        for i, (src, dst) in enumerate(
            [
                (mask_hbm, mask_ref),
                (q_hbm, q),
                (k_hbm, kb.at[0]),
                (lse_hbm, lse),
                (v_hbm, vb.at[0]),
                (o_hbm, o),
                (
                    g_hbm.at[:, pl.ds(pl.multiple_of(me * width, width), width)],
                    g.at[chunk_rows(me)],
                ),
            ]
        )
    ]
    for load in loads:
        load.start()

    barrier = pltpu.get_barrier_semaphore()
    for k in range(1, tp):
        pl.semaphore_signal(
            barrier, inc=1, device_id={"tp": lax.rem(me + k, tp)}, device_id_type=MESH
        )
    for d in range(1, n):
        pl.semaphore_signal(
            barrier, inc=1, device_id={"ctx": lax.rem(c + d, n)}, device_id_type=MESH
        )
    pl.semaphore_wait(barrier, tp - 1 + n - 1)

    def grad_copy(k):
        to = partner(me, k, tp)
        return pltpu.make_async_remote_copy(
            src_ref=g_hbm.at[:, pl.ds(pl.multiple_of(to * width, width), width)],
            dst_ref=g.at[chunk_rows(me)],
            send_sem=g_send.at[k - 1],
            recv_sem=g_recv.at[k - 1],
            device_id={"tp": to},
            device_id_type=MESH,
        )

    def grad_arrival(k):
        return pltpu.make_async_remote_copy(
            src_ref=g_hbm.at[:, pl.ds(0, width)],
            dst_ref=g.at[chunk_rows(source_of(me, k, tp))],
            send_sem=g_send.at[k - 1],
            recv_sem=g_recv.at[k - 1],
            device_id={"tp": source_of(me, k, tp)},
            device_id_type=MESH,
        )

    order = (1, 2, 3) if tp == 4 else tuple(range(1, tp))
    for k in order:
        grad_copy(k).start()

    def kv_copies(d):
        to = lax.rem(c + d, n)
        return [
            pltpu.make_async_remote_copy(
                src_ref=src,
                dst_ref=dst.at[d],
                send_sem=kv_send.at[i, d - 1],
                recv_sem=kv_recv.at[i, d - 1],
                device_id={"ctx": to},
                device_id_type=MESH,
            )
            for i, (src, dst) in enumerate([(k_hbm, kb), (v_hbm, vb)])
        ]

    for d in range(1, n):

        @pl.when(c + d < n)
        def _():
            for copy in kv_copies(d):
                copy.start()

    def stack(ref, s):
        return jnp.concatenate(
            [
                ref[chunk_rows(s), h * HEAD_SIZE : (h + 1) * HEAD_SIZE]
                for h in range(heads)
            ],
            axis=0,
        )

    def span_probs(slot, d, own):
        keys = kb[d]
        vx[slot, :, 0:HEAD_SIZE] = vb[d]
        key_at = lax.broadcasted_iota(jnp.int32, (rows, tokens), 1)
        row_at = lax.broadcasted_iota(jnp.int32, (rows, tokens), 0)
        key_block = key_at // BLK
        for s in range(tp):
            block = s // chunk_per_block
            table = jnp.zeros((rows, tokens), jnp.int32)
            for b in range(span_blocks if not own else block):
                allowed = mask_ref[c * span_blocks + block, (c - d) * span_blocks + b]
                table = jnp.where(key_block == b, allowed, table)
            live = table == 1
            if own:
                live = live | ((key_block == block) & (key_at <= row_at + s * rows))
            scores = dot(stack(q, s), keys, ((1,), (1,)))
            for h in range(heads):
                part = scores[h * rows : (h + 1) * rows] * scale
                col = lcol[s * rows : (s + 1) * rows, h : h + 1]
                p[slot, s, h * rows : (h + 1) * rows, :] = jnp.where(
                    live, jnp.exp(part - col), 0.0
                )
            pt[slot, s] = p[slot, s].T.astype(BF16)

    def chunk_lhs(s, grads):
        product = grads.astype(F32) * stack(o, s).astype(F32)
        high = product.astype(BF16)
        low = (product - high.astype(F32)).astype(BF16)
        lhs[s] = jnp.concatenate([grads, high, low], axis=1)

    def value_term(slot, s, grads):
        dva[slot] += dot(pt[slot, s], grads)

    def key_term(slot, s):
        inner = dot(lhs[s], vx[slot], ((1,), (1,)))
        dscore = (p[slot, s] * inner).astype(BF16)
        dkt[slot] += dot(qt[s], dscore)
        return dscore

    def chunk_terms(slot, d, s):
        value_term(slot, s, lhs[s, :, 0:HEAD_SIZE])
        return dot(key_term(slot, s), kb[d])

    def finish_query(s, total):
        grad = (total * scale).astype(BF16)
        for h in range(heads):
            dq_st[chunk_rows(s), h * HEAD_SIZE : (h + 1) * HEAD_SIZE] = grad[
                h * rows : (h + 1) * rows
            ]

    def partial_copies(d):
        to = lax.rem(c - d + n, n)
        return [
            pltpu.make_async_remote_copy(
                src_ref=src.at[d - 1],
                dst_ref=dst.at[d - 1],
                send_sem=d_send.at[i, d - 1],
                recv_sem=d_recv.at[i, d - 1],
                device_id={"ctx": to},
                device_id_type=MESH,
            )
            for i, (src, dst) in enumerate([(dk_send, dk_recv), (dv_send, dv_recv)])
        ]

    def send_value_partial(d):
        dv_send[d - 1] = dva[1].astype(BF16)
        partial_copies(d)[1].start()

    def send_key_partial(d):
        dk_send[d - 1] = dkt[1].astype(BF16)
        partial_copies(d)[0].start()

    dkt[...] = jnp.zeros_like(dkt)
    dva[...] = jnp.zeros_like(dva)
    dq_acc[...] = jnp.zeros_like(dq_acc)
    vx[:, :, HEAD_SIZE:] = jnp.full((2, tokens, 2 * HEAD_SIZE), -1.0, BF16)
    for load in loads:
        load.wait()
    lcol[...] = lse[...].T
    for s in range(tp):
        qt[s] = stack(q, s).T
    span_probs(0, 0, True)

    @pl.when(c >= 1)
    def _():
        for copy in kv_copies(1):
            copy.wait_recv()
        span_probs(1, 1, False)

    steps = (0,) + ((1, 2, 3) if tp == 4 else tuple(range(1, tp)))
    def own_terms(s):
        total = dq_acc[s] + chunk_terms(0, 0, s)
        if n == 2:
            finish_query(s, total)
        else:
            dq_acc[s] = total

    late = []
    for i, k in enumerate(steps):
        if k == 0:
            s = me
        else:
            s = source_of(me, k, tp)
            grad_arrival(k).wait_recv()
        grads = stack(g, s)
        if i < tp - 1:
            chunk_lhs(s, grads)

            @pl.when(c >= 1)
            def _():
                dq_acc[s] += chunk_terms(1, 1, s)

        else:
            @pl.when(c >= 1)
            def _():
                value_term(1, s, grads)
                send_value_partial(1)

            chunk_lhs(s, grads)

            @pl.when(c >= 1)
            def _():
                dscore = key_term(1, s)
                send_key_partial(1)
                dq_acc[s] += dot(dscore, kb[1])

        if i < tp - 2:
            own_terms(s)
        else:
            late.append(s)

    for s in late:
        own_terms(s)

    if n > 2:

        @pl.loop(2, n)
        def _(d):
            @pl.when(c >= d)
            def _():
                for copy in kv_copies(d):
                    copy.wait_recv()
                dkt[1] = jnp.zeros(dkt.shape[1:], F32)
                dva[1] = jnp.zeros(dva.shape[1:], F32)
                span_probs(1, d, False)
                for s in range(tp):
                    dq_acc[s] += chunk_terms(1, d, s)
                send_value_partial(d)
                send_key_partial(d)

        for s in range(tp):
            finish_query(s, dq_acc[s])

    for d in range(1, n):

        @pl.when(c + d < n)
        def _():
            keys_in, values_in = partial_copies(d)
            values_in.wait_recv()
            dva[0] += dv_recv[d - 1].astype(F32)
            keys_in.wait_recv()
            dkt[0] += dk_recv[d - 1].astype(F32)

    dk_st[...] = (dkt[0] * scale).T.astype(BF16)
    dv_st[...] = dva[0].astype(BF16)
    for k in range(1, tp):
        grad_copy(k).wait_send()
    for d in range(1, n):

        @pl.when(c + d < n)
        def _():
            for copy in kv_copies(d):
                copy.wait_send()

        @pl.when(c >= d)
        def _():
            for copy in partial_copies(d):
                copy.wait_send()


def local(query_rows, key_matrix, value_matrix, attn_out, out_grad, log_sums, block_mask):
    tokens, width = query_rows.shape
    heads = width // HEAD_SIZE
    n = lax.axis_size("ctx")
    tp = lax.axis_size("tp")
    rows = tokens // tp
    stacked = heads * rows
    vmem = pltpu.VMEM
    dma = pltpu.SemaphoreType.DMA
    hbm = pl.BlockSpec(memory_space=pltpu.HBM)
    return pl.pallas_call(
        functools.partial(kernel, n, tp),
        out_shape=(
            vmem((tokens, width), BF16),
            vmem((tokens, HEAD_SIZE), BF16),
            vmem((tokens, HEAD_SIZE), BF16),
        ),
        in_specs=[hbm] * 7,
        out_specs=(pl.BlockSpec(memory_space=pltpu.VMEM),) * 3,
        scratch_shapes=[
            vmem((tokens, width), BF16),
            vmem((tokens, width), BF16),
            vmem((tokens, width), BF16),
            vmem((heads, tokens), F32),
            vmem((n, tokens, HEAD_SIZE), BF16),
            vmem((n, tokens, HEAD_SIZE), BF16),
            vmem((2, tokens, 3 * HEAD_SIZE), BF16),
            vmem((tokens, heads), F32),
            vmem((tp, stacked, 3 * HEAD_SIZE), BF16),
            vmem((2, tp, stacked, tokens), F32),
            vmem((2, tp, tokens, stacked), BF16),
            vmem((tp, HEAD_SIZE, stacked), BF16),
            vmem((tp, stacked, HEAD_SIZE), F32),
            vmem((2, HEAD_SIZE, tokens), F32),
            vmem((2, tokens, HEAD_SIZE), F32),
            vmem((n - 1, HEAD_SIZE, tokens), BF16),
            vmem((n - 1, tokens, HEAD_SIZE), BF16),
            vmem((n - 1, HEAD_SIZE, tokens), BF16),
            vmem((n - 1, tokens, HEAD_SIZE), BF16),
            pltpu.SMEM(block_mask.shape, jnp.int32),
            dma((7,)),
            dma((tp - 1,)),
            dma((tp - 1,)),
            dma((2, n - 1)),
            dma((2, n - 1)),
            dma((2, n - 1)),
            dma((2, n - 1)),
        ],
        compiler_params=pltpu.CompilerParams(
            collective_id=0, has_side_effects=True, vmem_limit_bytes=62 * 1024 * 1024
        ),
    )(query_rows, key_matrix, value_matrix, attn_out, out_grad, log_sums, block_mask)


def solution(mesh):
    placed = (
        P(("dp", "ctx"), "tp"),
        P(("dp", "ctx"), "tp"),
        P(("dp", "ctx"), "tp"),
        P(("dp", "ctx"), "tp"),
        P(("dp", "ctx", "tp"), None),
        P("tp", ("dp", "ctx")),
        P("dp", None),
    )
    return jax.shard_map(
        local,
        mesh=mesh,
        in_specs=placed,
        out_specs=(P(("dp", "ctx"), "tp"), P(("dp", "ctx"), "tp"), P(("dp", "ctx"), "tp")),
        check_vma=False,
    )
```
